256 devices in a mesh: dp: 16 (over z_lo, x, core), row: 4 (over y), col: 4 (over z_hi).
Axes of the slice: x: 4, y: 4, z: 8 (z_hi: 4, z_lo: 2; z = z_hi * 2 + z_lo), core: 2. Of those that a mesh axis runs over, the one named last changes fastest.
Arguments:
- tokens: bfloat16 [2048, 4096], P(('dp', 'col'), 'row'), may hold values from -6 to 6
- up_weight: bfloat16 [4096, 8192], P('row', 'col'), may hold values from -0.09375 to 0.09375
- up_bias: float32 [8192], P('col'), may hold values from -3 to 3
- down_weight: bfloat16 [8192, 4096], P('col', 'row'), may hold values from -0.0625 to 0.0625
- out_grad: bfloat16 [2048, 4096], P(('dp', 'col'), 'row'), may hold values from -6 to 6
- bucket_lengths: int32 [64], P(('dp', 'col')), may hold values from 1 to 32, as said below
Outputs:
- input_grad: bfloat16 [2048, 4096], P(('dp', 'col'), 'row')
- up_weight_grad: float32 [4096, 4, 2048], P('row', 'col', 'dp')
- up_bias_grad: float32 [4, 2048], P('col', 'dp')
- down_weight_grad: float32 [4, 2048, 4096], P('col', 'dp', 'row')
The draws below stay inside these ranges and needn't reach their ends.
Inputs may be any that keep to these rules, and one draw needn't show every extreme that they name: `bucket_lengths`: some block is full.
All inputs are finite; a program needn't handle non-finite values.
Results may differ from the reference program's by a relative error of at most 0.0055.
Values may be sent and summed in bfloat16 or wider, within the bound.
No kernel may reach another device: no remote copies, remote signals or barrier semaphores. Data moves between devices by JAX's collectives and lax.ppermute only.
A program may use at most 128 MiB of HBM per device.

```python
import math
import jax
import jax.numpy as jnp
from jax import lax

D = 4096
FF = 8192
CAP = 32
TOKENS = 2048
FF_TILE = 2048
N_COL = 4


def draw_bucket_lengths(key, part):
    count = TOKENS // CAP
    first_key = jax.random.fold_in(key, 11)
    second_key = jax.random.fold_in(key, 23)
    lengths = jax.random.randint(first_key, (count,), 1, CAP + 1, dtype=jnp.int32)
    full_block = jax.random.randint(second_key, (), 0, count, dtype=jnp.int32)
    return jnp.where(jnp.arange(count, dtype=jnp.int32) == full_block, CAP, lengths).astype(jnp.int32)


def level_of(own_key, shape, split, low, high):
    level, own = 1.0, jax.random.fold_in(own_key, 6)
    for dim, blocks in split:
        steps = jnp.exp(jax.random.uniform(jax.random.fold_in(own, dim), (blocks,), jnp.float32, low / len(split), high / len(split)))
        level = level * jnp.repeat(steps, shape[dim] // blocks).reshape([-1 if axis == dim else 1 for axis in range(len(shape))])
    return level


def normal_values(rng, shape, width, bound, pieces=(), kind=jnp.bfloat16):
    loudness = level_of(rng, shape, pieces, -0.22, 0.18) if pieces else 1.0
    result = jax.random.normal(rng, shape, jnp.float32) * width * loudness
    return jnp.minimum(jnp.maximum(result, -bound), bound).astype(kind)


def setup_inputs(seed: int = 0) -> dict:
    seeds = jax.random.split(jax.random.key(seed), 7)
    tokens = normal_values(seeds[0], (TOKENS, D), 1.0, 6.0, ((0, 64), (1, 4)))
    up_weight = normal_values(seeds[1], (D, FF), D ** -0.5, 0.09375, ((0, 4), (1, 4)))
    up_bias = normal_values(seeds[2], (FF,), 0.5, 3.0, ((0, 4),), jnp.float32)
    down_weight = normal_values(seeds[3], (FF, D), FF ** -0.5, 0.0625, ((0, 4), (1, 4)))
    out_grad = normal_values(seeds[4], (TOKENS, D), 1.0, 6.0, ((0, 64), (1, 4)))
    bucket_lengths = draw_bucket_lengths(jax.random.fold_in(seeds[6], 71), 0)
    return dict(tokens=tokens, up_weight=up_weight, up_bias=up_bias, down_weight=down_weight, out_grad=out_grad, bucket_lengths=bucket_lengths)


coef = math.sqrt(2.0 / math.pi)

def gelu_pair(pre):
    inner = coef * (pre + 0.044715 * pre * pre * pre)
    tanh_val = jnp.tanh(inner)
    value = 0.5 * pre * (1.0 + tanh_val)
    slope = 0.5 * (1.0 + tanh_val) + 0.5 * pre * (1.0 - tanh_val * tanh_val) * coef * (1.0 + 3.0 * 0.044715 * pre * pre)
    return (value, slope)

def reference(tokens, up_weight, up_bias, down_weight, out_grad, bucket_lengths):
    position = jnp.arange(TOKENS, dtype=jnp.int32)
    limits = jnp.repeat(bucket_lengths, CAP, total_repeat_length=TOKENS)
    live = position % CAP < limits
    masked = jnp.where(live[:, None], out_grad, jnp.zeros_like(out_grad))
    pre = jnp.dot(tokens, up_weight, preferred_element_type=jnp.float32) + up_bias[None, :]
    value, slope = gelu_pair(pre)
    act = value.astype(jnp.bfloat16)
    act_grad = jnp.dot(masked, down_weight.T, preferred_element_type=jnp.float32)
    pre_grad = (act_grad * slope).astype(jnp.bfloat16)
    down_grad = jnp.dot(act.T, masked, preferred_element_type=jnp.float32)
    up_grad = jnp.dot(tokens.T, pre_grad, preferred_element_type=jnp.float32)
    bias_grad = lax.optimization_barrier(jnp.sum(pre_grad.astype(jnp.float32), axis=0))
    input_grad = jnp.dot(pre_grad, up_weight.T, preferred_element_type=jnp.float32).astype(jnp.bfloat16)
    return (input_grad, up_grad.reshape(D, N_COL, FF_TILE), bias_grad.reshape(N_COL, FF_TILE), down_grad.reshape(N_COL, FF_TILE, D))
```

```python
import math

import jax
import jax.numpy as jnp
from jax import lax
from jax.sharding import PartitionSpec as P

coef = math.sqrt(2.0 / math.pi)


def gelu_pair(pre):
    inner = coef * (pre + 0.044715 * pre * pre * pre)
    tanh_val = jnp.tanh(inner)
    value = 0.5 * pre * (1.0 + tanh_val)
    slope = 0.5 * (1.0 + tanh_val) + 0.5 * pre * (1.0 - tanh_val * tanh_val) * coef * (
        1.0 + 3.0 * 0.044715 * pre * pre
    )
    return (value, slope)


def dot(left, right, dims):
    return lax.dot_general(left, right, (dims, ((), ())), preferred_element_type=jnp.float32)


def sum_parts(parts):
    return jnp.sum(parts.astype(jnp.float32), axis=0)


def spread(array, axis):
    count = lax.axis_size(axis)
    return lax.all_to_all(jnp.broadcast_to(array[None], (count, *array.shape)), axis, 0, 0)


def local(tokens, up_weight, up_bias, down_weight, out_grad, bucket_lengths):
    rows, width = out_grad.shape
    hidden = up_weight.shape[1]
    n_dp, n_row, n_col = lax.axis_size("dp"), lax.axis_size("row"), lax.axis_size("col")
    blocks = bucket_lengths.shape[0]
    block_rows = rows // blocks
    position = jnp.arange(rows, dtype=jnp.int32)
    limits = jnp.repeat(bucket_lengths, block_rows, total_repeat_length=rows)
    live = position % block_rows < limits
    masked = jnp.where(live[:, None], out_grad, jnp.zeros_like(out_grad))
    both = jnp.concatenate([tokens, masked], axis=1)
    group = lax.all_gather(both, "col", axis=0, tiled=True)
    group_all = lax.all_gather(group, "dp", axis=0, tiled=True)

    pre_part = dot(group[:, :width], up_weight, ((1,), (0,))).astype(jnp.bfloat16)
    act_grad_part = dot(group[:, width:], down_weight, ((1,), (1,))).astype(jnp.bfloat16)
    parts = jnp.concatenate(
        [pre_part.reshape(n_row, rows, hidden), act_grad_part.reshape(n_row, rows, hidden)], axis=1
    )
    sums = sum_parts(lax.all_to_all(parts, "row", 0, 0))
    value, slope = gelu_pair(sums[:rows] + up_bias[None, :])
    act = value.astype(jnp.bfloat16)
    pre_grad = (sums[rows:] * slope).astype(jnp.bfloat16)

    narrow = hidden // n_dp
    pair = jnp.stack([act, pre_grad]).reshape(2, rows, n_dp, narrow).transpose(2, 0, 1, 3)
    pair = lax.all_to_all(pair, "dp", 0, 0)
    pair_all = spread(pair, "row")
    pair_all = pair_all.transpose(2, 1, 0, 3, 4).reshape(2, n_dp * n_row * rows, narrow)
    act_all, pre_grad_all = pair_all[0], pair_all[1]

    pre_grad_group = spread(pre_grad, "row").reshape(n_row * rows, hidden)
    input_part = dot(pre_grad_group, up_weight, ((1,), (1,))).astype(jnp.bfloat16)
    input_grad = sum_parts(
        lax.all_to_all(input_part.reshape(n_col, rows, width), "col", 0, 0)
    ).astype(jnp.bfloat16)

    up_grad = dot(group_all[:, :width], pre_grad_all, ((0,), (0,)))
    down_grad = dot(act_all, group_all[:, width:], ((0,), (0,)))
    bias_grad = jnp.sum(pre_grad_all.astype(jnp.float32), axis=0)
    return (
        input_grad,
        up_grad.reshape(width, 1, narrow),
        bias_grad.reshape(1, narrow),
        down_grad.reshape(1, narrow, width),
    )


def solution(mesh):
    return jax.shard_map(
        local,
        mesh=mesh,
        in_specs=(
            P(("dp", "col"), "row"),
            P("row", "col"),
            P("col"),
            P("col", "row"),
            P(("dp", "col"), "row"),
            P(("dp", "col")),
        ),
        out_specs=(
            P(("dp", "col"), "row"),
            P("row", "col", "dp"),
            P("col", "dp"),
            P("col", "dp", "row"),
        ),
        check_vma=False,
    )
```

```python
import math

import jax
import jax.numpy as jnp
from jax import lax
from jax.experimental import pallas as pl
from jax.experimental.pallas import tpu as pltpu
from jax.sharding import PartitionSpec as P

coef = math.sqrt(2.0 / math.pi)
ZL, NX, NC = 2, 4, 2
PEERS = ZL * NX
SIDE = 4
MASK, GELU, INPUT, WEIGHT = 64, 32, 64, 64
VMEM = pl.BlockSpec(memory_space=pltpu.VMEM)
SMEM = pl.BlockSpec(memory_space=pltpu.SMEM)
bf16, f32 = jnp.bfloat16, jnp.float32


def gelu_pair(pre):
    inner = coef * (pre + 0.044715 * pre * pre * pre)
    tanh_val = jnp.tanh(inner)
    value = 0.5 * pre * (1.0 + tanh_val)
    slope = 0.5 * (1.0 + tanh_val) + 0.5 * pre * (1.0 - tanh_val * tanh_val) * coef * (
        1.0 + 3.0 * 0.044715 * pre * pre
    )
    return (value, slope)


def dot(left, right, dims):
    return lax.dot_general(left, right, (dims, ((), ())), preferred_element_type=f32)


def shape(dims, kind):
    return jax.ShapeDtypeStruct(dims, kind)


def call(kernel, outs, scratch, cost, *args, smem=0, tail=0, name=None):
    return pl.pallas_call(
        kernel,
        out_shape=outs,
        in_specs=[SMEM] * smem + [VMEM] * (len(args) - smem),
        out_specs=(VMEM,) * (len(outs) - tail) + (SMEM,) * tail,
        scratch_shapes=scratch,
        compiler_params=pltpu.CompilerParams(vmem_limit_bytes=24 << 20),
        cost_estimate=pl.CostEstimate(flops=cost[0], bytes_accessed=cost[1], transcendentals=0),
        name=name,
    )(*args)


def shift(array, axis, by):
    count = lax.axis_size(axis)
    return lax.ppermute(array, axis, [(i, (i + by) % count) for i in range(count)])


def move(array, step):
    pairs = []
    for z in range(ZL):
        for x in range(NX):
            for c in range(NC):
                tz, tx, tc = step(z, x, c)
                pairs.append(((z * NX + x) * NC + c, (tz * NX + tx) * NC + tc))
    return lax.ppermute(array, "dp", pairs)


def shift_x(array, by):
    return move(array, lambda z, x, c: (z, (x + by) % NX, c))


def flip_z(array):
    return move(array, lambda z, x, c: (1 - z, x, c))


def flip_core(array):
    return move(array, lambda z, x, c: (z, x, 1 - c))


def mask_kernel(lengths, tokens, out_grad, both):
    rows, width = tokens.shape
    live = lax.broadcasted_iota(jnp.int32, (rows, width), 0) < lengths[0]
    both[:, :width] = tokens[...]
    both[:, width:] = jnp.where(live, out_grad[...], jnp.zeros_like(out_grad))


def near_kernel(place, up, down, same):
    for i in range(4):
        same[i] = place[i]


def first_kernel(place, b0, b1, b2, b3, up, down, group, keep, s1, s2, s3, parts):
    rows, both = b0.shape
    width, hidden = up.shape
    row = place[0]
    for k, block in enumerate((b0, b1, b2, b3)):
        group[k * rows : (k + 1) * rows, :] = block[...]
    tile = 512
    for t in range(hidden // tile):
        at = slice(t * tile, (t + 1) * tile)
        pre = dot(group[:, :width], up[:, at], ((1,), (0,)))
        act = dot(group[:, width:], down[at, :], ((1,), (1,)))
        for k in range(SIDE):
            own = slice(k * rows, (k + 1) * rows)
            parts[k, :rows, at] = pre[own]
            parts[k, rows:, at] = act[own]
    keep[...] = parts[row]
    for k, send in ((1, s1), (2, s2), (3, s3)):
        send[...] = parts[lax.rem(row + k, SIDE)].astype(bf16)


def gelu_kernel(keep, r1, r2, r3, bias, pair, pre_grad):
    rows = keep.shape[0] // 2
    wide = pair.shape[2]
    for p in range(PEERS):
        at = slice(p * wide, (p + 1) * wide)
        total = keep[:, at] + r1[:, at].astype(f32) + r2[:, at].astype(f32) + r3[:, at].astype(f32)
        value, slope = gelu_pair(total[:rows] + bias[:, at])
        grad = (total[rows:] * slope).astype(bf16)
        pair[p, :rows, :] = value.astype(bf16)
        pair[p, rows:, :] = grad
        pre_grad[:, at] = grad


def input_kernel(place, g0, g1, g2, g3, up, keep, s1, s2, s3, same, parts):
    rows = g0.shape[0]
    row = place[0]
    for i in range(4):
        same[i] = place[i]
    group = jnp.concatenate([g0[...], g1[...], g2[...], g3[...]], axis=0)
    tile = 256
    for t in range(up.shape[0] // tile):
        at = slice(t * tile, (t + 1) * tile)
        term = dot(group, up[at, :], ((1,), (1,)))
        for k in range(SIDE):
            parts[k, :, at] = term[k * rows : (k + 1) * rows]
    keep[...] = parts[row]
    for k, send in ((1, s1), (2, s2), (3, s3)):
        send[...] = parts[lax.rem(row + (SIDE - k), SIDE)].astype(bf16)


def weight_kernel(place, *refs):
    pieces, pairs = refs[:8], refs[8:12]
    up_keep, down_keep, bias_keep, send = refs[12:16]
    act_s, grad_s = refs[16:18]
    row, x, z, core = place[0], place[1], place[2], place[3]
    whole = pieces[0].shape[0]
    rows = whole // SIDE
    spot = {0: 0, 1: 1, 3: 2}
    for m in range(SIDE):
        block = lax.rem(row + (SIDE - m), SIDE)
        for dz in range(ZL):
            for dx in range(NX):
                peer = lax.rem(z + dz, ZL) * NX + lax.rem(x + (NX - dx), NX)
                if dx == 2:
                    at = (6 * whole + dz * (whole // 2)) + (
                        lax.div(block, 2) * whole + lax.rem(block, 2) * rows
                    )
                else:
                    at = (dz * 3 + spot[dx]) * whole + block * rows
                at = pl.multiple_of(at, rows)
                act_s[pl.ds(at, rows), :] = pairs[m][peer, :rows, :]
                grad_s[pl.ds(at, rows), :] = pairs[m][peer, rows:, :]
    narrow, width = up_keep.shape
    own = pl.multiple_of(core * narrow, narrow)
    other = pl.multiple_of((1 - core) * narrow, narrow)
    send[2 * narrow :, :] = jnp.zeros((send.shape[0] - 2 * narrow, width), f32)
    for at, out, i in ((own, bias_keep, 0), (other, send, 2 * narrow)):
        total = jnp.sum(grad_s[:, pl.ds(at, narrow)].astype(f32), axis=0, keepdims=True)
        out[i : i + 1, :narrow] = total
    tile = 256
    for scratch, offset, keep, to in (
        (grad_s, 0, up_keep, 0),
        (act_s, width, down_keep, narrow),
    ):
        left = jnp.concatenate(
            [scratch[:, pl.ds(own, narrow)].T, scratch[:, pl.ds(other, narrow)].T], axis=0
        )
        for t in range(width // tile):
            at = slice(t * tile, (t + 1) * tile)
            src = slice(offset + t * tile, offset + (t + 1) * tile)
            acc = None
            for q in range(4):
                right = jnp.concatenate([pieces[2 * q][:, src], pieces[2 * q + 1][:, src]], axis=0)
                term = dot(left[:, q * 2 * whole : (q + 1) * 2 * whole], right, ((1,), (0,)))
                acc = term if acc is None else acc + term
            keep[:, at] = acc[:narrow]
            send[to : to + narrow, at] = acc[narrow:]


def last_kernel(up_keep, down_keep, bias_keep, got, keep, i1, i2, i3, up, down, bias, inp):
    inp[...] = (
        keep[...] + i1[...].astype(f32) + i2[...].astype(f32) + i3[...].astype(f32)
    ).astype(bf16)
    narrow = up_keep.shape[0]
    up[...] = (up_keep[...] + got[:narrow, :]).T
    down[...] = down_keep[...] + got[narrow : 2 * narrow, :]
    bias[...] = bias_keep[...] + got[2 * narrow : 2 * narrow + 1, :narrow]


def local(tokens, up_weight, up_bias, down_weight, out_grad, bucket_lengths):
    rows, width = out_grad.shape
    hidden = up_weight.shape[1]
    narrow = hidden // (PEERS * NC)
    row = lax.axis_index("row")
    dp = lax.axis_index("dp")
    core, x, z = dp % NC, (dp // NC) % NX, dp // (NC * NX)
    place = jnp.stack([row, x, z, core]).astype(jnp.int32)

    (both,) = call(
        mask_kernel,
        (shape((rows, 2 * width), bf16),),
        (),
        (0, MASK << 20),
        bucket_lengths,
        tokens,
        out_grad,
        smem=1,
        name="mask",
    )
    (place,) = call(
        near_kernel,
        (shape((4,), jnp.int32),),
        (),
        (0, 1 << 20),
        place,
        up_weight,
        down_weight,
        smem=1,
        tail=1,
        name="near",
    )
    c2 = shift(both, "col", 2)
    c1, c3 = shift(both, "col", 1), shift(both, "col", 3)
    send = shape((2 * rows, hidden), bf16)
    group, keep, s1, s2, s3 = call(
        first_kernel,
        (shape((SIDE * rows, 2 * width), bf16), shape((2 * rows, hidden), f32), send, send, send),
        [pltpu.VMEM((SIDE, 2 * rows, hidden), f32)],
        (8 * SIDE * rows * width * hidden, 8 << 20),
        place,
        both,
        c1,
        c2,
        c3,
        up_weight,
        down_weight,
        smem=1,
        name="first",
    )
    r2 = shift(s2, "row", 2)
    r1, r3 = shift(s1, "row", 1), shift(s3, "row", 3)

    half = SIDE * rows // 2
    other = flip_z(group)
    after, before = shift_x(group, 1), shift_x(group, -1)

    pair, pre_grad = call(
        gelu_kernel,
        (shape((PEERS, 2 * rows, NC * narrow), bf16), shape((rows, hidden), bf16)),
        (),
        (1 << 22, GELU << 20),
        keep,
        r1,
        r2,
        r3,
        up_bias.reshape(1, hidden),
        name="gelu",
    )
    other, pre_grad = lax.optimization_barrier((other, pre_grad))
    after_o, before_o = shift_x(other, 1), shift_x(other, -1)
    groups = [[NC * p + c for p in range(PEERS)] for c in range(NC)]
    pair = lax.all_to_all(pair, "dp", 0, 0, axis_index_groups=groups)
    g2 = shift(pre_grad, "row", 2)
    g1, g3 = shift(pre_grad, "row", 1), shift(pre_grad, "row", 3)
    after_o, before_o, g1, g2, g3 = lax.optimization_barrier((after_o, before_o, g1, g2, g3))
    far_a = shift_x(jnp.concatenate([after[:half], after_o[:half]], axis=0), 1)
    far_b = shift_x(jnp.concatenate([before[half:], before_o[half:]], axis=0), -1)
    pieces = [group, after, before, other, after_o, before_o, far_a, far_b]
    p2 = shift(pair, "row", 2)
    p1, p3 = shift(pair, "row", 1), shift(pair, "row", 3)

    send = shape((rows, width), bf16)
    keep, s1, s2, s3, place = call(
        input_kernel,
        (shape((rows, width), f32), send, send, send, shape((4,), jnp.int32)),
        [pltpu.VMEM((SIDE, rows, width), f32)],
        (2 * SIDE * rows * width * hidden, INPUT << 20),
        place,
        pre_grad,
        g1,
        g2,
        g3,
        up_weight,
        smem=1,
        tail=1,
        name="input",
    )
    i2 = shift(s2, "col", -2)
    i1, i3 = shift(s1, "col", -1), shift(s3, "col", -3)

    block, line = shape((narrow, width), f32), shape((1, narrow), f32)
    count = PEERS * SIDE * rows
    up_keep, down_keep, bias_keep, send = call(
        weight_kernel,
        (block, block, line, shape((2 * narrow + 8, width), f32)),
        [pltpu.VMEM((count, NC * narrow), bf16)] * 2,
        (8 * count * width * narrow * NC, WEIGHT << 20),
        place,
        *pieces,
        pair,
        p1,
        p2,
        p3,
        smem=1,
        name="weight",
    )
    send, i1, i2, i3 = lax.optimization_barrier((send, i1, i2, i3))
    up_grad, down_grad, bias_grad, input_grad = call(
        last_kernel,
        (shape((width, narrow), f32), block, line, shape((rows, width), bf16)),
        (),
        (1 << 20, 3 << 20),
        up_keep,
        down_keep,
        bias_keep,
        flip_core(send),
        keep,
        i1,
        i2,
        i3,
        name="last",
    )
    return (
        input_grad,
        up_grad.reshape(width, 1, narrow),
        bias_grad,
        down_grad.reshape(1, narrow, width),
    )


def solution(mesh):
    return jax.shard_map(
        local,
        mesh=mesh,
        in_specs=(
            P(("dp", "col"), "row"),
            P("row", "col"),
            P("col"),
            P("col", "row"),
            P(("dp", "col"), "row"),
            P(("dp", "col")),
        ),
        out_specs=(
            P(("dp", "col"), "row"),
            P("row", "col", "dp"),
            P("col", "dp"),
            P("col", "dp", "row"),
        ),
        check_vma=False,
    )
```

```python
import math

import jax
import jax.numpy as jnp
from jax import lax
from jax.experimental import pallas as pl
from jax.experimental.pallas import tpu as pltpu
from jax.sharding import PartitionSpec as P

coef = math.sqrt(2.0 / math.pi)
ZL, NX, NC = 2, 4, 2
PEERS = ZL * NX
SIDE = 4
MASK, GELU, INPUT, WEIGHT = 64, 32, 64, 64
VMEM = pl.BlockSpec(memory_space=pltpu.VMEM)
SMEM = pl.BlockSpec(memory_space=pltpu.SMEM)
bf16, f32 = jnp.bfloat16, jnp.float32


def gelu_pair(pre):
    inner = coef * (pre + 0.044715 * pre * pre * pre)
    tanh_val = jnp.tanh(inner)
    value = 0.5 * pre * (1.0 + tanh_val)
    slope = 0.5 * (1.0 + tanh_val) + 0.5 * pre * (1.0 - tanh_val * tanh_val) * coef * (
        1.0 + 3.0 * 0.044715 * pre * pre
    )
    return (value, slope)


def dot(left, right, dims):
    return lax.dot_general(left, right, (dims, ((), ())), preferred_element_type=f32)


def shape(dims, kind):
    return jax.ShapeDtypeStruct(dims, kind)


def call(kernel, outs, scratch, cost, *args, smem=0, tail=0, name=None):
    return pl.pallas_call(
        kernel,
        out_shape=outs,
        in_specs=[SMEM] * smem + [VMEM] * (len(args) - smem),
        out_specs=(VMEM,) * (len(outs) - tail) + (SMEM,) * tail,
        scratch_shapes=scratch,
        compiler_params=pltpu.CompilerParams(vmem_limit_bytes=24 << 20),
        cost_estimate=pl.CostEstimate(flops=cost[0], bytes_accessed=cost[1], transcendentals=0),
        name=name,
    )(*args)


def shift(array, axis, by):
    count = lax.axis_size(axis)
    return lax.ppermute(array, axis, [(i, (i + by) % count) for i in range(count)])


def move(array, step):
    pairs = []
    for z in range(ZL):
        for x in range(NX):
            for c in range(NC):
                tz, tx, tc = step(z, x, c)
                pairs.append(((z * NX + x) * NC + c, (tz * NX + tx) * NC + tc))
    return lax.ppermute(array, "dp", pairs)


def shift_x(array, by):
    return move(array, lambda z, x, c: (z, (x + by) % NX, c))


def flip_z(array):
    return move(array, lambda z, x, c: (1 - z, x, c))


def flip_core(array):
    return move(array, lambda z, x, c: (z, x, 1 - c))


def near_kernel(place, up, down, same):
    for i in range(4):
        same[i] = place[i]


def first_kernel(place, b0, b1, b2, b3, up, down, group, keep, send, parts):
    rows, both = b0.shape
    width, hidden = up.shape
    row = place[0]
    for k, block in enumerate((b0, b1, b2, b3)):
        group[k * rows : (k + 1) * rows, :] = block[...]
    tile = 512
    for t in range(hidden // tile):
        at = slice(t * tile, (t + 1) * tile)
        pre = dot(group[:, :width], up[:, at], ((1,), (0,)))
        act = dot(group[:, width:], down[at, :], ((1,), (1,)))
        for k in range(SIDE):
            own = slice(k * rows, (k + 1) * rows)
            parts[k, :rows, at] = pre[own]
            parts[k, rows:, at] = act[own]
    keep[...] = parts[row]
    send[...] = parts[...].astype(bf16)


def gelu_kernel(place, keep, got, bias, pair, pre_grad):
    others = [lax.rem(place[0] + k, SIDE) for k in (1, 2, 3)]
    rows = keep.shape[0] // 2
    wide = pair.shape[2]
    for p in range(PEERS):
        at = slice(p * wide, (p + 1) * wide)
        total = keep[:, at]
        for other in others:
            total = total + got[other, :, at].astype(f32)
        value, slope = gelu_pair(total[:rows] + bias[:, at])
        grad = (total[rows:] * slope).astype(bf16)
        pair[p, :rows, :] = value.astype(bf16)
        pair[p, rows:, :] = grad
        pre_grad[:, at] = grad


def input_kernel(place, g0, g1, g2, g3, up, keep, s1, s2, s3, same, parts):
    rows = g0.shape[0]
    row = place[0]
    for i in range(4):
        same[i] = place[i]
    group = jnp.concatenate([g0[...], g1[...], g2[...], g3[...]], axis=0)
    tile = 256
    for t in range(up.shape[0] // tile):
        at = slice(t * tile, (t + 1) * tile)
        term = dot(group, up[at, :], ((1,), (1,)))
        for k in range(SIDE):
            parts[k, :, at] = term[k * rows : (k + 1) * rows]
    keep[...] = parts[row]
    for k, send in ((1, s1), (2, s2), (3, s3)):
        send[...] = parts[lax.rem(row + (SIDE - k), SIDE)].astype(bf16)


def weight_kernel(place, *refs):
    pieces, pairs = refs[:8], refs[8:12]
    up_keep, down_keep, bias_keep, send = refs[12:16]
    act_s, grad_s = refs[16:18]
    row, x, z, core = place[0], place[1], place[2], place[3]
    whole = pieces[0].shape[0]
    rows = whole // SIDE
    spot = {0: 0, 1: 1, 3: 2}
    for m in range(SIDE):
        block = lax.rem(row + (SIDE - m), SIDE)
        for dz in range(ZL):
            for dx in range(NX):
                peer = lax.rem(z + dz, ZL) * NX + lax.rem(x + (NX - dx), NX)
                if dx == 2:
                    at = (6 * whole + dz * (whole // 2)) + (
                        lax.div(block, 2) * whole + lax.rem(block, 2) * rows
                    )
                else:
                    at = (dz * 3 + spot[dx]) * whole + block * rows
                at = pl.multiple_of(at, rows)
                act_s[pl.ds(at, rows), :] = pairs[m][peer, :rows, :]
                grad_s[pl.ds(at, rows), :] = pairs[m][peer, rows:, :]
    narrow, width = up_keep.shape
    own = pl.multiple_of(core * narrow, narrow)
    other = pl.multiple_of((1 - core) * narrow, narrow)
    send[2 * narrow :, :] = jnp.zeros((send.shape[0] - 2 * narrow, width), f32)
    for at, out, i in ((own, bias_keep, 0), (other, send, 2 * narrow)):
        total = jnp.sum(grad_s[:, pl.ds(at, narrow)].astype(f32), axis=0, keepdims=True)
        out[i : i + 1, :narrow] = total
    tile = 256
    for scratch, offset, keep, to in (
        (grad_s, 0, up_keep, 0),
        (act_s, width, down_keep, narrow),
    ):
        left = jnp.concatenate(
            [scratch[:, pl.ds(own, narrow)].T, scratch[:, pl.ds(other, narrow)].T], axis=0
        )
        for t in range(width // tile):
            at = slice(t * tile, (t + 1) * tile)
            src = slice(offset + t * tile, offset + (t + 1) * tile)
            acc = None
            for q in range(4):
                right = jnp.concatenate([pieces[2 * q][:, src], pieces[2 * q + 1][:, src]], axis=0)
                term = dot(left[:, q * 2 * whole : (q + 1) * 2 * whole], right, ((1,), (0,)))
                acc = term if acc is None else acc + term
            keep[:, at] = acc[:narrow]
            send[to : to + narrow, at] = acc[narrow:]


def last_kernel(up_keep, down_keep, bias_keep, got, keep, i1, i2, i3, up, down, bias, inp):
    inp[...] = (
        keep[...] + i1[...].astype(f32) + i2[...].astype(f32) + i3[...].astype(f32)
    ).astype(bf16)
    narrow = up_keep.shape[0]
    up[...] = (up_keep[...] + got[:narrow, :]).T
    down[...] = down_keep[...] + got[narrow : 2 * narrow, :]
    bias[...] = bias_keep[...] + got[2 * narrow : 2 * narrow + 1, :narrow]


def local(tokens, up_weight, up_bias, down_weight, out_grad, bucket_lengths):
    rows, width = out_grad.shape
    hidden = up_weight.shape[1]
    narrow = hidden // (PEERS * NC)
    row = lax.axis_index("row")
    dp = lax.axis_index("dp")
    core, x, z = dp % NC, (dp // NC) % NX, dp // (NC * NX)
    place = jnp.stack([row, x, z, core]).astype(jnp.int32)

    live = lax.broadcasted_iota(jnp.int32, (rows, 2 * width), 0) < bucket_lengths[0]
    live = live | (lax.broadcasted_iota(jnp.int32, (rows, 2 * width), 1) < width)
    both = jnp.where(live, jnp.concatenate([tokens, out_grad], axis=1), jnp.zeros((), bf16))
    (place,) = call(
        near_kernel,
        (shape((4,), jnp.int32),),
        (),
        (0, 1 << 20),
        place,
        up_weight,
        down_weight,
        smem=1,
        tail=1,
        name="near",
    )
    c2 = shift(both, "col", 2)
    c1, c3 = shift(both, "col", 1), shift(both, "col", 3)
    send = shape((SIDE, 2 * rows, hidden), bf16)
    group, keep, send = call(
        first_kernel,
        (shape((SIDE * rows, 2 * width), bf16), shape((2 * rows, hidden), f32), send),
        [pltpu.VMEM((SIDE, 2 * rows, hidden), f32)],
        (8 * SIDE * rows * width * hidden, 8 << 20),
        place,
        both,
        c1,
        c2,
        c3,
        up_weight,
        down_weight,
        smem=1,
        name="first",
    )
    got = lax.all_to_all(send, "row", 0, 0)

    half = SIDE * rows // 2
    other = flip_z(group)
    after, before = shift_x(group, 1), shift_x(group, -1)

    pair, pre_grad = call(
        gelu_kernel,
        (shape((PEERS, 2 * rows, NC * narrow), bf16), shape((rows, hidden), bf16)),
        (),
        (1 << 22, GELU << 20),
        place,
        keep,
        got,
        up_bias.reshape(1, hidden),
        smem=1,
        name="gelu",
    )
    other, pre_grad = lax.optimization_barrier((other, pre_grad))
    after_o, before_o = shift_x(other, 1), shift_x(other, -1)
    groups = [[NC * p + c for p in range(PEERS)] for c in range(NC)]
    pair = lax.all_to_all(pair, "dp", 0, 0, axis_index_groups=groups)
    g2 = shift(pre_grad, "row", 2)
    g1, g3 = shift(pre_grad, "row", 1), shift(pre_grad, "row", 3)
    after_o, before_o, g1, g2, g3, pair = lax.optimization_barrier(
        (after_o, before_o, g1, g2, g3, pair)
    )
    far_a = shift_x(jnp.concatenate([after[:half], after_o[:half]], axis=0), 1)
    far_b = shift_x(jnp.concatenate([before[half:], before_o[half:]], axis=0), -1)
    pieces = [group, after, before, other, after_o, before_o, far_a, far_b]
    p2 = shift(pair, "row", 2)
    p1, p3 = shift(pair, "row", 1), shift(pair, "row", 3)

    send = shape((rows, width), bf16)
    keep, s1, s2, s3, place = call(
        input_kernel,
        (shape((rows, width), f32), send, send, send, shape((4,), jnp.int32)),
        [pltpu.VMEM((SIDE, rows, width), f32)],
        (2 * SIDE * rows * width * hidden, INPUT << 20),
        place,
        pre_grad,
        g1,
        g2,
        g3,
        up_weight,
        smem=1,
        tail=1,
        name="input",
    )
    i2 = shift(s2, "col", -2)
    i1, i3 = shift(s1, "col", -1), shift(s3, "col", -3)

    block, line = shape((narrow, width), f32), shape((1, narrow), f32)
    count = PEERS * SIDE * rows
    up_keep, down_keep, bias_keep, send = call(
        weight_kernel,
        (block, block, line, shape((2 * narrow + 8, width), f32)),
        [pltpu.VMEM((count, NC * narrow), bf16)] * 2,
        (8 * count * width * narrow * NC, WEIGHT << 20),
        place,
        *pieces,
        pair,
        p1,
        p2,
        p3,
        smem=1,
        name="weight",
    )
    send, i1, i2, i3 = lax.optimization_barrier((send, i1, i2, i3))
    up_grad, down_grad, bias_grad, input_grad = call(
        last_kernel,
        (shape((width, narrow), f32), block, line, shape((rows, width), bf16)),
        (),
        (1 << 20, 3 << 20),
        up_keep,
        down_keep,
        bias_keep,
        flip_core(send),
        keep,
        i1,
        i2,
        i3,
        name="last",
    )
    return (
        input_grad,
        up_grad.reshape(width, 1, narrow),
        bias_grad,
        down_grad.reshape(1, narrow, width),
    )


def solution(mesh):
    return jax.shard_map(
        local,
        mesh=mesh,
        in_specs=(
            P(("dp", "col"), "row"),
            P("row", "col"),
            P("col"),
            P("col", "row"),
            P(("dp", "col"), "row"),
            P(("dp", "col")),
        ),
        out_specs=(
            P(("dp", "col"), "row"),
            P("row", "col", "dp"),
            P("col", "dp"),
            P("col", "dp", "row"),
        ),
        check_vma=False,
    )
```

```python
import math

import jax
import jax.numpy as jnp
from jax import lax
from jax.experimental import pallas as pl
from jax.experimental.pallas import tpu as pltpu
from jax.sharding import PartitionSpec as P

coef = math.sqrt(2.0 / math.pi)
ZL, NX, NC = 2, 4, 2
PEERS = ZL * NX
SIDE = 4
MASK, GELU, INPUT, WEIGHT = 64, 32, 64, 64
VMEM = pl.BlockSpec(memory_space=pltpu.VMEM)
SMEM = pl.BlockSpec(memory_space=pltpu.SMEM)
bf16, f32 = jnp.bfloat16, jnp.float32


def gelu_pair(pre):
    inner = coef * (pre + 0.044715 * pre * pre * pre)
    tanh_val = jnp.tanh(inner)
    value = 0.5 * pre * (1.0 + tanh_val)
    slope = 0.5 * (1.0 + tanh_val) + 0.5 * pre * (1.0 - tanh_val * tanh_val) * coef * (
        1.0 + 3.0 * 0.044715 * pre * pre
    )
    return (value, slope)


def dot(left, right, dims):
    return lax.dot_general(left, right, (dims, ((), ())), preferred_element_type=f32)


def shape(dims, kind):
    return jax.ShapeDtypeStruct(dims, kind)


def call(kernel, outs, scratch, cost, *args, smem=0, tail=0, name=None):
    return pl.pallas_call(
        kernel,
        out_shape=outs,
        in_specs=[SMEM] * smem + [VMEM] * (len(args) - smem),
        out_specs=(VMEM,) * (len(outs) - tail) + (SMEM,) * tail,
        scratch_shapes=scratch,
        compiler_params=pltpu.CompilerParams(vmem_limit_bytes=24 << 20),
        cost_estimate=pl.CostEstimate(flops=cost[0], bytes_accessed=cost[1], transcendentals=0),
        name=name,
    )(*args)


def shift(array, axis, by):
    count = lax.axis_size(axis)
    return lax.ppermute(array, axis, [(i, (i + by) % count) for i in range(count)])


def move(array, step):
    pairs = []
    for z in range(ZL):
        for x in range(NX):
            for c in range(NC):
                tz, tx, tc = step(z, x, c)
                pairs.append(((z * NX + x) * NC + c, (tz * NX + tx) * NC + tc))
    return lax.ppermute(array, "dp", pairs)


def shift_x(array, by):
    return move(array, lambda z, x, c: (z, (x + by) % NX, c))


def flip_z(array):
    return move(array, lambda z, x, c: (1 - z, x, c))


def flip_core(array):
    return move(array, lambda z, x, c: (z, x, 1 - c))


def near_kernel(place, up, down, same):
    for i in range(4):
        same[i] = place[i]


def first_kernel(place, b0, b1, b2, b3, up, down, group, keep, send, parts):
    rows, both = b0.shape
    width, hidden = up.shape
    row = place[0]
    for k, block in enumerate((b0, b1, b2, b3)):
        group[k * rows : (k + 1) * rows, :] = block[...]
    tile = 512
    for t in range(hidden // tile):
        at = slice(t * tile, (t + 1) * tile)
        pre = dot(group[:, :width], up[:, at], ((1,), (0,)))
        act = dot(group[:, width:], down[at, :], ((1,), (1,)))
        for k in range(SIDE):
            own = slice(k * rows, (k + 1) * rows)
            parts[k, :rows, at] = pre[own]
            parts[k, rows:, at] = act[own]
    keep[...] = parts[row]
    send[...] = parts[...].astype(bf16)


def gelu_kernel(place, keep, got, bias, pair, pre_grad):
    others = [lax.rem(place[0] + k, SIDE) for k in (1, 2, 3)]
    rows = keep.shape[0] // 2
    wide = pair.shape[2]
    for p in range(PEERS):
        at = slice(p * wide, (p + 1) * wide)
        total = keep[:, at]
        for other in others:
            total = total + got[other, :, at].astype(f32)
        value, slope = gelu_pair(total[:rows] + bias[:, at])
        grad = (total[rows:] * slope).astype(bf16)
        pair[p, :rows, :] = value.astype(bf16)
        pair[p, rows:, :] = grad
        pre_grad[:, at] = grad


def input_kernel(place, g0, g1, g2, g3, up, keep, s1, s2, s3, same, parts):
    rows = g0.shape[0]
    row = place[0]
    for i in range(4):
        same[i] = place[i]
    group = jnp.concatenate([g0[...], g1[...], g2[...], g3[...]], axis=0)
    tile = 256
    for t in range(up.shape[0] // tile):
        at = slice(t * tile, (t + 1) * tile)
        term = dot(group, up[at, :], ((1,), (1,)))
        for k in range(SIDE):
            parts[k, :, at] = term[k * rows : (k + 1) * rows]
    keep[...] = parts[row]
    for k, send in ((1, s1), (2, s2), (3, s3)):
        send[...] = parts[lax.rem(row + (SIDE - k), SIDE)].astype(bf16)


def weight_kernel(place, *refs):
    pieces, pairs = refs[:8], refs[8:12]
    up_keep, down_keep, bias_keep, up_send, down_send = refs[12:17]
    act_s, grad_s = refs[17:19]
    row, x, z, core = place[0], place[1], place[2], place[3]
    whole = pieces[0].shape[0]
    rows = whole // SIDE
    spot = {0: 0, 1: 1, 3: 2}
    for m in range(SIDE):
        block = lax.rem(row + (SIDE - m), SIDE)
        for dz in range(ZL):
            for dx in range(NX):
                peer = lax.rem(z + dz, ZL) * NX + lax.rem(x + (NX - dx), NX)
                if dx == 2:
                    at = (6 * whole + dz * (whole // 2)) + (
                        lax.div(block, 2) * whole + lax.rem(block, 2) * rows
                    )
                else:
                    at = (dz * 3 + spot[dx]) * whole + block * rows
                at = pl.multiple_of(at, rows)
                act_s[pl.ds(at, rows), :] = pairs[m][peer, :rows, :]
                grad_s[pl.ds(at, rows), :] = pairs[m][peer, rows:, :]
    narrow, width = up_keep.shape
    own = pl.multiple_of(core * narrow, narrow)
    other = pl.multiple_of((1 - core) * narrow, narrow)
    up_send[narrow:, :] = jnp.zeros((up_send.shape[0] - narrow, width), f32)
    for at, out, i in ((own, bias_keep, 0), (other, up_send, narrow)):
        total = jnp.sum(grad_s[:, pl.ds(at, narrow)].astype(f32), axis=0, keepdims=True)
        out[i : i + 1, :narrow] = total
    tile = 256
    for scratch, offset, keep, send in (
        (grad_s, 0, up_keep, up_send),
        (act_s, width, down_keep, down_send),
    ):
        left = jnp.concatenate(
            [scratch[:, pl.ds(own, narrow)].T, scratch[:, pl.ds(other, narrow)].T], axis=0
        )
        for t in range(width // tile):
            at = slice(t * tile, (t + 1) * tile)
            src = slice(offset + t * tile, offset + (t + 1) * tile)
            acc = None
            for q in range(4):
                right = jnp.concatenate([pieces[2 * q][:, src], pieces[2 * q + 1][:, src]], axis=0)
                term = dot(left[:, q * 2 * whole : (q + 1) * 2 * whole], right, ((1,), (0,)))
                acc = term if acc is None else acc + term
            keep[:, at] = acc[:narrow]
            send[:narrow, at] = acc[narrow:]


def last_kernel(
    up_keep, down_keep, bias_keep, up_got, down_got, keep, i1, i2, i3, up, down, bias, inp
):
    inp[...] = (
        keep[...] + i1[...].astype(f32) + i2[...].astype(f32) + i3[...].astype(f32)
    ).astype(bf16)
    narrow = up_keep.shape[0]
    up[...] = (up_keep[...] + up_got[:narrow, :]).T
    down[...] = down_keep[...] + down_got[...]
    bias[...] = bias_keep[...] + up_got[narrow : narrow + 1, :narrow]


def local(tokens, up_weight, up_bias, down_weight, out_grad, bucket_lengths):
    rows, width = out_grad.shape
    hidden = up_weight.shape[1]
    narrow = hidden // (PEERS * NC)
    row = lax.axis_index("row")
    dp = lax.axis_index("dp")
    core, x, z = dp % NC, (dp // NC) % NX, dp // (NC * NX)
    place = jnp.stack([row, x, z, core]).astype(jnp.int32)

    live = lax.broadcasted_iota(jnp.int32, (rows, 2 * width), 0) < bucket_lengths[0]
    live = live | (lax.broadcasted_iota(jnp.int32, (rows, 2 * width), 1) < width)
    both = jnp.where(live, jnp.concatenate([tokens, out_grad], axis=1), jnp.zeros((), bf16))
    (place,) = call(
        near_kernel,
        (shape((4,), jnp.int32),),
        (),
        (0, 1 << 20),
        place,
        up_weight,
        down_weight,
        smem=1,
        tail=1,
        name="near",
    )
    c2 = shift(both, "col", 2)
    c1, c3 = shift(both, "col", 1), shift(both, "col", 3)
    send = shape((SIDE, 2 * rows, hidden), bf16)
    group, keep, send = call(
        first_kernel,
        (shape((SIDE * rows, 2 * width), bf16), shape((2 * rows, hidden), f32), send),
        [pltpu.VMEM((SIDE, 2 * rows, hidden), f32)],
        (8 * SIDE * rows * width * hidden, 8 << 20),
        place,
        both,
        c1,
        c2,
        c3,
        up_weight,
        down_weight,
        smem=1,
        name="first",
    )
    got = lax.all_to_all(send, "row", 0, 0)

    half = SIDE * rows // 2
    other = flip_z(group)
    after, before = shift_x(group, 1), shift_x(group, -1)

    pair, pre_grad = call(
        gelu_kernel,
        (shape((PEERS, 2 * rows, NC * narrow), bf16), shape((rows, hidden), bf16)),
        (),
        (1 << 22, GELU << 20),
        place,
        keep,
        got,
        up_bias.reshape(1, hidden),
        smem=1,
        name="gelu",
    )
    other, pre_grad = lax.optimization_barrier((other, pre_grad))
    after_o, before_o = shift_x(other, 1), shift_x(other, -1)
    groups = [[NC * p + c for p in range(PEERS)] for c in range(NC)]
    pair = lax.all_to_all(pair, "dp", 0, 0, axis_index_groups=groups)
    g2 = shift(pre_grad, "row", 2)
    g1, g3 = shift(pre_grad, "row", 1), shift(pre_grad, "row", 3)
    after_o, before_o, g1, g2, g3, pair = lax.optimization_barrier(
        (after_o, before_o, g1, g2, g3, pair)
    )
    far_a = shift_x(jnp.concatenate([after[:half], after_o[:half]], axis=0), 1)
    far_b = shift_x(jnp.concatenate([before[half:], before_o[half:]], axis=0), -1)
    pieces = [group, after, before, other, after_o, before_o, far_a, far_b]
    p2 = shift(pair, "row", 2)
    p1, p3 = shift(pair, "row", 1), shift(pair, "row", 3)

    send = shape((rows, width), bf16)
    keep, s1, s2, s3, place = call(
        input_kernel,
        (shape((rows, width), f32), send, send, send, shape((4,), jnp.int32)),
        [pltpu.VMEM((SIDE, rows, width), f32)],
        (2 * SIDE * rows * width * hidden, INPUT << 20),
        place,
        pre_grad,
        g1,
        g2,
        g3,
        up_weight,
        smem=1,
        tail=1,
        name="input",
    )
    i2 = shift(s2, "col", -2)
    i1, i3 = shift(s1, "col", -1), shift(s3, "col", -3)

    block, line = shape((narrow, width), f32), shape((1, narrow), f32)
    count = PEERS * SIDE * rows
    up_keep, down_keep, bias_keep, up_send, down_send = call(
        weight_kernel,
        (block, block, line, shape((narrow + 8, width), f32), block),
        [pltpu.VMEM((count, NC * narrow), bf16)] * 2,
        (8 * count * width * narrow * NC, WEIGHT << 20),
        place,
        *pieces,
        pair,
        p1,
        p2,
        p3,
        smem=1,
        name="weight",
    )
    down_send, i1, i2, i3 = lax.optimization_barrier((down_send, i1, i2, i3))
    up_grad, down_grad, bias_grad, input_grad = call(
        last_kernel,
        (shape((width, narrow), f32), block, line, shape((rows, width), bf16)),
        (),
        (1 << 20, 3 << 20),
        up_keep,
        down_keep,
        bias_keep,
        flip_core(up_send),
        flip_core(down_send),
        keep,
        i1,
        i2,
        i3,
        name="last",
    )
    return (
        input_grad,
        up_grad.reshape(width, 1, narrow),
        bias_grad,
        down_grad.reshape(1, narrow, width),
    )


def solution(mesh):
    return jax.shard_map(
        local,
        mesh=mesh,
        in_specs=(
            P(("dp", "col"), "row"),
            P("row", "col"),
            P("col"),
            P("col", "row"),
            P(("dp", "col"), "row"),
            P(("dp", "col")),
        ),
        out_specs=(
            P(("dp", "col"), "row"),
            P("row", "col", "dp"),
            P("col", "dp"),
            P("col", "dp", "row"),
        ),
        check_vma=False,
    )
```
